32 devices in a mesh: pole: 2 (over y), prow: 4 (over z), pcol: 4 (over x, core).
Axes of the slice: x: 2, y: 2, z: 4, core: 2. Of those that a mesh axis runs over, the one named last changes fastest.
Arguments:
- ainv: bfloat16 [4, 1024, 1024], P('pole', 'prow', 'pcol'), parts along dimension 0, may hold values from -0.1875 to 0.1875
- panel: bfloat16 [4, 4, 4, 64, 256], P('pole', 'pcol', 'prow'), parts along dimension 0, may hold values from -6 to 6
- upanel: bfloat16 [4, 256, 1024], P('pole', None, 'prow'), parts along dimension 0, may hold values from -0.1875 to 0.1875
- dinv: float32 [4, 256, 256], P('pole'), parts along dimension 0, may hold values from -6 to 6
- pattern: int32 [8, 8], P('prow', 'pcol'), may hold values from 0 to 1, as said below
Outputs:
- column: bfloat16 [4, 1024, 256], P('pole', 'prow'), parts along dimension 0
- diagonal: float32 [4, 256, 256], P('pole'), parts along dimension 0
The draws below stay inside these ranges and needn't reach their ends.
There are 2 independent parts, one for each index of `pole`. The reference program is written for one: setup_inputs(seed, part) draws one part's arguments, and reference() takes and returns one part's arrays. A program takes and returns all parts, laid end to end along the dimension named above; an argument that names none is the same for every part. Nothing has to cross between parts.
Inputs may be any that keep to these rules, and one draw needn't show every extreme that they name: pattern[i, i] = 1 for every block i; the number of present blocks varies from row to row.
All inputs are finite; a program needn't handle non-finite values.
Results may differ from the reference program's by a relative error of at most 0.0004.
Values may be sent and summed in bfloat16 or wider, within the bound.
A program may use at most 64 MiB of HBM per device.

```python
import jax
import jax.numpy as jnp
from jax import lax

W = 256
BLK = 128
NBLK = 8
N = 1024
PR = 64
N_PROW = 4
N_PCOL = 4


def draw_pattern(key, part):
    key = jax.random.fold_in(key, 7)
    first, second = jax.random.split(key)
    density = jax.random.randint(first, (NBLK, 1), 1, 9)
    levels = jax.random.randint(second, (NBLK, NBLK), 0, 8)
    present = (levels < density).astype(jnp.int32)
    return jnp.maximum(present, jnp.eye(NBLK, dtype=jnp.int32))


def level_of(stream_key, dims, shards, low, top_value):
    gain = 1.0
    for position, shards_of in shards:
        heights = jax.random.uniform(jax.random.fold_in(jax.random.fold_in(stream_key, 6), position), (shards_of,), jnp.float32, low / len(shards), top_value / len(shards))
        gain = gain * jnp.repeat(jnp.exp(heights), dims[position] // shards_of).reshape((-1,) + (1,) * (len(dims) - 1 - position))
    return gain


def gaussian(stream_key, dims, deviation, most, shards=(), kind=jnp.bfloat16):
    level = level_of(stream_key, dims, shards, -0.22, 0.18) if shards else 1.0
    values = jax.random.normal(stream_key, dims, jnp.float32) * deviation * level
    return jnp.minimum(jnp.maximum(values, -most), most).astype(kind)


def setup_inputs(seed: int = 0, part: int = 0) -> dict:
    key_of = jax.random.split(jax.random.key(seed), 6)
    part_keys = jax.random.split(jax.random.fold_in(key_of[5], part), 6)
    return {
        "ainv": gaussian(part_keys[0], (2, N, N), N ** -0.5, 0.1875, ((1, 4), (2, 4))),
        "panel": gaussian(part_keys[1], (2, N_PCOL, N_PROW, PR, W), 1.0, 6.0, ((1, 4), (2, 4))),
        "upanel": gaussian(part_keys[2], (2, W, N), N ** -0.5, 0.1875, ((2, 4),)),
        "dinv": gaussian(part_keys[3], (2, W, W), 1.0, 6.0, (), jnp.float32),
        "pattern": draw_pattern(jax.random.fold_in(key_of[5], 71), part),
    }


def complex_dot(left_re, left_im, right_re, right_im):
    real = jnp.dot(left_re, right_re, preferred_element_type=jnp.float32) - jnp.dot(left_im, right_im, preferred_element_type=jnp.float32)
    imag = jnp.dot(left_re, right_im, preferred_element_type=jnp.float32) + jnp.dot(left_im, right_re, preferred_element_type=jnp.float32)
    return real, imag


def reference(ainv, panel, upanel, dinv, pattern):
    blocks = pattern.shape[0]
    weights = pattern.astype(jnp.bfloat16)
    masked = (ainv.reshape(2, blocks, BLK, blocks, BLK) * weights[None, :, None, :, None]).reshape(ainv.shape)
    lower = panel.reshape(2, N, W)
    real, imag = complex_dot(masked[0], masked[1], lower[0], lower[1])
    column_full = jnp.stack([-real, -imag])
    column = column_full.astype(jnp.bfloat16)
    up_full = upanel.astype(jnp.float32)
    hi = lax.Precision.HIGHEST
    d_re = jnp.dot(up_full[0], column_full[0], precision=hi) - jnp.dot(up_full[1], column_full[1], precision=hi)
    d_im = jnp.dot(up_full[0], column_full[1], precision=hi) + jnp.dot(up_full[1], column_full[0], precision=hi)
    diagonal = dinv - jnp.stack([d_re, d_im])
    return column, diagonal
```

```python
import functools

import jax
import jax.numpy as jnp
from jax import lax
from jax.experimental import pallas as pl
from jax.experimental.pallas import tpu as pltpu
from jax.sharding import PartitionSpec as P

BLK = 128
MESH = pl.DeviceIdType.MESH
F32 = jnp.float32
BF16 = jnp.bfloat16


def kernel(n, ainv, panel, upanel, dinv, pattern, col_out, diag_out,
           a_v, u_v, d_v, low, m_v, um_v, part, core_in, cx, tbuf, x_in, xc_in,
           sbuf, z_in, dall, call,
           loc_sem, p_send, p_recv, b_send, b_recv, x_send, x_recv, z_send, z_recv,
           gz_send, gz_recv, gx_send, gx_recv, gc_send, gc_recv, c_send, c_recv):
    pole = lax.axis_index("pole")
    me = lax.axis_index("prow")
    j = lax.axis_index("pcol")
    h = lax.rem(j, 2)
    x = j // 2
    rows = panel.shape[3]
    z_peer = [lax.rem(me + d, n) for d in range(n)]
    z_from = [lax.rem(me + n - d, n) for d in range(n)]
    sib = (pole, me, j + 1 - 2 * h)
    xp = (pole, me, lax.rem(j + 2, 4))

    def remote(src, dst, send, recv, device):
        return pltpu.make_async_remote_copy(
            src_ref=src, dst_ref=dst, send_sem=send, recv_sem=recv,
            device_id=device, device_id_type=MESH)

    my_rows = pl.ds(pl.multiple_of(me * rows, rows), rows)
    locs = [
        pltpu.make_async_copy(panel.at[:, 0, 0], low.at[:, my_rows], loc_sem.at[0]),
        pltpu.make_async_copy(ainv, a_v, loc_sem.at[1]),
        pltpu.make_async_copy(upanel, u_v, loc_sem.at[2]),
        pltpu.make_async_copy(dinv, d_v, loc_sem.at[3]),
    ]
    for c in locs:
        c.start()
    barrier = pltpu.get_barrier_semaphore()
    others = [(pole, z_peer[d], j) for d in range(1, n)] + [sib, xp]
    for dev in others:
        pl.semaphore_signal(barrier, inc=1, device_id=dev, device_id_type=MESH)
    pl.semaphore_wait(barrier, len(others))

    sends = []
    gathers = []
    for d in range(1, n):
        c = remote(panel.at[:, 0, 0], low.at[:, my_rows], p_send.at[d], p_recv.at[d],
                   (pole, z_peer[d], j))
        c.start()
        gathers.append(c)
        sends.append(c)

    locs[1].wait()
    w = a_v.shape[2]
    for bi in range(pattern.shape[0]):
        for bj in range(pattern.shape[1]):
            wt = pattern[bi, bj].astype(F32)
            rs = slice(bi * BLK, (bi + 1) * BLK)
            cs = slice(bj * BLK, (bj + 1) * BLK)
            r0, c0 = bi * BLK, bj * BLK
            re = a_v[0, rs, cs].astype(F32) * wt
            im = a_v[1, rs, cs].astype(F32) * wt
            nre = (-re).astype(BF16)
            m_v[r0:r0 + BLK, c0:c0 + BLK] = nre
            m_v[w + r0:w + r0 + BLK, w + c0:w + c0 + BLK] = nre
            m_v[r0:r0 + BLK, w + c0:w + c0 + BLK] = im.astype(BF16)
            m_v[w + r0:w + r0 + BLK, c0:c0 + BLK] = (-im).astype(BF16)
    locs[2].wait()
    um_v[:w, :w] = u_v[0]
    um_v[w:, w:] = u_v[0]
    um_v[:w, w:] = -u_v[1]
    um_v[w:, :w] = u_v[1]
    locs[0].wait()
    for c in gathers:
        c.wait_recv()

    prod = jnp.dot(m_v[...], low[...].reshape(2 * w, w), preferred_element_type=F32)
    part[0] = prod[:, :BLK]
    part[1] = prod[:, BLK:]
    c = remote(part.at[1 - h], core_in, b_send, b_recv, sib)
    c.start()
    c.wait_recv()
    sends.append(c)

    half = part[h] + core_in[...]
    cx[...] = half.reshape(cx.shape)
    hi = half.astype(BF16)
    lo = (half - hi.astype(F32)).astype(BF16)
    t = jnp.dot(um_v[...], jnp.concatenate([hi, lo], axis=1), preferred_element_type=F32)
    tbuf[...] = (t[:, :BLK] + t[:, BLK:]).reshape(tbuf.shape)
    dx = remote(tbuf.at[:, 1 - x], x_in, x_send.at[0], x_recv.at[0], xp)
    dx.start()
    cxc = remote(cx.at[:, 1 - x], xc_in, x_send.at[1], x_recv.at[1], xp)
    cxc.start()
    sends += [dx, cxc]
    dx.wait_recv()
    sbuf[...] = tbuf[:, x] + x_in[...]
    zs = []
    for d in range(1, n):
        c = remote(sbuf.at[:, z_peer[d]], z_in.at[d], z_send.at[d], z_recv.at[d],
                   (pole, z_peer[d], j))
        c.start()
        zs.append(c)
    sends += zs

    cxc.wait_recv()
    call[h, x] = (cx[:, x] + xc_in[...]).astype(BF16)
    col_x = remote(call.at[h, x], call.at[h, x], c_send.at[0], c_recv.at[0], xp)
    col_s = remote(call.at[h, x], call.at[h, x], c_send.at[1], c_recv.at[1], sib)
    col_x.start()
    col_s.start()
    sends += [col_x, col_s]

    total = sbuf[:, me]
    for d in range(1, n):
        zs[d - 1].wait_recv()
        total = total + z_in[d]
    dall[h, x, me] = total

    def piece(side, d, dev, send, recv):
        slot = dall.at[h, side, z_from[d]]
        c = remote(slot, slot, send, recv, dev)
        c.start()
        sends.append(c)
        return c

    mine = dall.at[h, x, me]
    gz = []
    for d in range(1, n):
        c = remote(mine, mine, gz_send.at[d], gz_recv.at[d], (pole, z_peer[d], j))
        c.start()
        sends.append(c)
        gz.append(c)
    gx = [piece(x, 0, xp, gx_send.at[0], gx_recv.at[0])]
    gc = [piece(x, 0, sib, gc_send.at[0], gc_recv.at[0])]

    col_x.wait_recv()
    other = call.at[h, 1 - x]
    col_f = remote(other, other, c_send.at[2], c_recv.at[2], sib)
    col_f.start()
    sends.append(col_f)

    for d in range(1, n):
        gz[d - 1].wait_recv()
        gx.append(piece(x, d, xp, gx_send.at[d], gx_recv.at[d]))
        gc.append(piece(x, d, sib, gc_send.at[d], gc_recv.at[d]))
    for d in range(n):
        gx[d].wait_recv()
        gc.append(piece(1 - x, d, sib, gc_send.at[n + d], gc_recv.at[n + d]))

    col_s.wait_recv()
    col_f.wait_recv()
    for a in range(2):
        for b in range(2):
            col_out[:, b * BLK:(b + 1) * BLK, a * BLK:(a + 1) * BLK] = call[a, b]
    locs[3].wait()
    for c in gc:
        c.wait_recv()
    pr = dall.shape[4]
    for a in range(2):
        for b in range(2):
            for k in range(n):
                rs = slice(b * BLK + k * pr, b * BLK + (k + 1) * pr)
                cs = slice(a * BLK, (a + 1) * BLK)
                diag_out[:, rs, cs] = d_v[:, rs, cs] - dall[a, b, k]
    for c in sends:
        c.wait_send()


def fused(n, ainv, panel, upanel, dinv, pattern):
    w = ainv.shape[2]
    pr = BLK // n
    dma = pltpu.SemaphoreType.DMA
    hbm = pl.BlockSpec(memory_space=pl.ANY)
    vmem = pl.BlockSpec(memory_space=pltpu.VMEM)
    return pl.pallas_call(
        functools.partial(kernel, n),
        out_shape=(
            jax.ShapeDtypeStruct((2, w, w), BF16),
            jax.ShapeDtypeStruct((2, w, w), F32),
        ),
        in_specs=[hbm, hbm, hbm, hbm, pl.BlockSpec(memory_space=pltpu.SMEM)],
        out_specs=(vmem, vmem),
        scratch_shapes=[
            pltpu.VMEM((2, w, w), BF16),
            pltpu.VMEM((2, w, w), BF16),
            pltpu.VMEM((2, w, w), F32),
            pltpu.VMEM((2, w, w), BF16),
            pltpu.VMEM((2 * w, 2 * w), BF16),
            pltpu.VMEM((2 * w, 2 * w), BF16),
            pltpu.VMEM((2, 2 * w, BLK), F32),
            pltpu.VMEM((2 * w, BLK), F32),
            pltpu.VMEM((2, 2, BLK, BLK), F32),
            pltpu.VMEM((2, 2, n, pr, BLK), F32),
            pltpu.VMEM((2, n, pr, BLK), F32),
            pltpu.VMEM((2, BLK, BLK), F32),
            pltpu.VMEM((2, n, pr, BLK), F32),
            pltpu.VMEM((n, 2, pr, BLK), F32),
            pltpu.VMEM((2, 2, n, 2, pr, BLK), F32),
            pltpu.VMEM((2, 2, 2, BLK, BLK), BF16),
            dma((4,)),
            dma((n,)), dma((n,)),
            dma, dma,
            dma((2,)), dma((2,)),
            dma((n,)), dma((n,)),
            dma((n,)), dma((n,)),
            dma((n,)), dma((n,)),
            dma((2 * n,)), dma((2 * n,)),
            dma((3,)), dma((3,)),
        ],
        compiler_params=pltpu.CompilerParams(
            collective_id=0, has_side_effects=True, vmem_limit_bytes=48 * 2**20),
        cost_estimate=pl.CostEstimate(
            flops=12 * w**3, bytes_accessed=12 * w * w, transcendentals=0),
    )(ainv, panel, upanel, dinv, pattern)


def complex_dot(left_re, left_im, right_re, right_im):
    real = jnp.dot(left_re, right_re, preferred_element_type=F32) - jnp.dot(
        left_im, right_im, preferred_element_type=F32
    )
    imag = jnp.dot(left_re, right_im, preferred_element_type=F32) + jnp.dot(
        left_im, right_re, preferred_element_type=F32
    )
    return (real, imag)


def upper_terms(up_full, column_full):
    hi = lax.Precision.HIGHEST
    d_re = jnp.dot(up_full[0], column_full[0], precision=hi) - jnp.dot(
        up_full[1], column_full[1], precision=hi
    )
    d_im = jnp.dot(up_full[0], column_full[1], precision=hi) + jnp.dot(
        up_full[1], column_full[0], precision=hi
    )
    return jnp.stack([d_re, d_im])


def general(ainv, panel, upanel, dinv, pattern):
    local_cols = ainv.shape[2]
    row_blocks = pattern.shape[0]
    col_blocks = pattern.shape[1]
    width = panel.shape[4]
    weights = pattern.astype(BF16)
    masked = (
        ainv.reshape(2, row_blocks, BLK, col_blocks, BLK) * weights[None, :, None, :, None]
    ).reshape(ainv.shape)
    gathered = lax.all_gather(panel, "prow", axis=2, tiled=True).reshape(2, local_cols, width)
    real, imag = complex_dot(masked[0], masked[1], gathered[0], gathered[1])
    column_full = lax.psum(jnp.stack([-real, -imag]), "pcol")
    column = column_full.astype(BF16)
    total = lax.psum(upper_terms(upanel.astype(F32), column_full), "prow")
    return (column, dinv - total)


def solution(mesh):
    n = mesh.shape["prow"]

    def per_device(ainv, panel, upanel, dinv, pattern):
        square = ainv.shape[1:] == (2 * BLK, 2 * BLK) and panel.shape[4] == 2 * BLK
        if n == 4 and mesh.shape["pcol"] == 4 and square:
            return fused(n, ainv, panel, upanel, dinv, pattern)
        return general(ainv, panel, upanel, dinv, pattern)

    in_specs = (
        P("pole", "prow", "pcol"),
        P("pole", "pcol", "prow", None, None),
        P("pole", None, "prow"),
        P("pole", None, None),
        P("prow", "pcol"),
    )
    out_specs = (P("pole", "prow", None), P("pole", None, None))
    return jax.shard_map(
        per_device, mesh=mesh, in_specs=in_specs, out_specs=out_specs, check_vma=False
    )
```

```python
import functools

import jax
import jax.numpy as jnp
from jax import lax
from jax.experimental import pallas as pl
from jax.experimental.pallas import tpu as pltpu
from jax.sharding import PartitionSpec as P

BLK = 128
MESH = pl.DeviceIdType.MESH
F32 = jnp.float32
BF16 = jnp.bfloat16


def kernel(n, ainv, panel, upanel, dinv, pattern, col_out, diag_out,
           pat_s, a_v, u_v, d_v, low, m_v, um_v, part, core_in, cx, tbuf, x_in, xc_in,
           sbuf, z_in, dall, call,
           loc_sem, p_send, p_recv, b_send, b_recv, x_send, x_recv, z_send, z_recv,
           gz_send, gz_recv, gx_send, gx_recv, gc_send, gc_recv, c_send, c_recv):
    pole = lax.axis_index("pole")
    me = lax.axis_index("prow")
    j = lax.axis_index("pcol")
    h = lax.rem(j, 2)
    x = j // 2
    rows = panel.shape[3]
    z_peer = [lax.rem(me + d, n) for d in range(n)]
    z_from = [lax.rem(me + n - d, n) for d in range(n)]
    sib = (pole, me, j + 1 - 2 * h)
    xp = (pole, me, lax.rem(j + 2, 4))

    def remote(src, dst, send, recv, device):
        return pltpu.make_async_remote_copy(
            src_ref=src, dst_ref=dst, send_sem=send, recv_sem=recv,
            device_id=device, device_id_type=MESH)

    my_rows = pl.ds(pl.multiple_of(me * rows, rows), rows)
    locs = [
        pltpu.make_async_copy(panel.at[:, 0, 0], low.at[:, my_rows], loc_sem.at[0]),
        pltpu.make_async_copy(ainv, a_v, loc_sem.at[1]),
        pltpu.make_async_copy(upanel, u_v, loc_sem.at[2]),
        pltpu.make_async_copy(dinv, d_v, loc_sem.at[3]),
        pltpu.make_async_copy(pattern, pat_s, loc_sem.at[4]),
    ]
    for c in locs:
        c.start()
    barrier = pltpu.get_barrier_semaphore()
    others = [(pole, z_peer[d], j) for d in range(1, n)] + [sib, xp]
    for dev in others:
        pl.semaphore_signal(barrier, inc=1, device_id=dev, device_id_type=MESH)
    pl.semaphore_wait(barrier, len(others))

    sends = []
    gathers = []
    for d in range(1, n):
        c = remote(panel.at[:, 0, 0], low.at[:, my_rows], p_send.at[d], p_recv.at[d],
                   (pole, z_peer[d], j))
        c.start()
        gathers.append(c)
        sends.append(c)

    locs[1].wait()
    locs[4].wait()
    w = a_v.shape[2]
    for bi in range(pattern.shape[0]):
        for bj in range(pattern.shape[1]):
            wt = pat_s[bi, bj].astype(F32)
            rs = slice(bi * BLK, (bi + 1) * BLK)
            cs = slice(bj * BLK, (bj + 1) * BLK)
            r0, c0 = bi * BLK, bj * BLK
            re = a_v[0, rs, cs].astype(F32) * wt
            im = a_v[1, rs, cs].astype(F32) * wt
            nre = (-re).astype(BF16)
            m_v[r0:r0 + BLK, c0:c0 + BLK] = nre
            m_v[w + r0:w + r0 + BLK, w + c0:w + c0 + BLK] = nre
            m_v[r0:r0 + BLK, w + c0:w + c0 + BLK] = im.astype(BF16)
            m_v[w + r0:w + r0 + BLK, c0:c0 + BLK] = (-im).astype(BF16)
    locs[2].wait()
    um_v[:w, :w] = u_v[0]
    um_v[w:, w:] = u_v[0]
    um_v[:w, w:] = -u_v[1]
    um_v[w:, :w] = u_v[1]
    locs[0].wait()
    for c in gathers:
        c.wait_recv()

    prod = jnp.dot(m_v[...], low[...].reshape(2 * w, w), preferred_element_type=F32)
    part[0] = prod[:, :BLK]
    part[1] = prod[:, BLK:]
    c = remote(part.at[1 - h], core_in, b_send, b_recv, sib)
    c.start()
    c.wait_recv()
    sends.append(c)

    half = part[h] + core_in[...]
    cx[...] = half.reshape(cx.shape)
    hi = half.astype(BF16)
    lo = (half - hi.astype(F32)).astype(BF16)
    t = jnp.dot(um_v[...], jnp.concatenate([hi, lo], axis=1), preferred_element_type=F32)
    tbuf[...] = (t[:, :BLK] + t[:, BLK:]).reshape(tbuf.shape)
    dx = []
    for c in range(2):
        dx.append(remote(tbuf.at[c, 1 - x], x_in.at[c], x_send.at[c], x_recv.at[c], xp))
        dx[c].start()
    cxc = remote(cx.at[:, 1 - x], xc_in, x_send.at[2], x_recv.at[2], xp)
    cxc.start()
    sends += dx + [cxc]
    zs = []
    for c in range(2):
        dx[c].wait_recv()
        sbuf[c] = tbuf[c, x] + x_in[c]
        for d in range(1, n):
            s = c * n + d
            zs.append(remote(sbuf.at[c, z_peer[d]], z_in.at[c, d], z_send.at[s],
                             z_recv.at[s], (pole, z_peer[d], j)))
            zs[-1].start()
    sends += zs

    def piece(side, d, c, dev, send, recv):
        slot = dall.at[h, side, z_from[d], c]
        copy = remote(slot, slot, send, recv, dev)
        copy.start()
        sends.append(copy)
        return copy

    gz, gx, gc = [], {}, []
    for c in range(2):
        total = sbuf[c, me]
        for d in range(1, n):
            zs[c * (n - 1) + d - 1].wait_recv()
            total = total + z_in[c, d]
        dall[h, x, me, c] = total
        for d in range(1, n):
            s = c * n + d
            gz.append(piece(x, 0, c, (pole, z_peer[d], j), gz_send.at[s], gz_recv.at[s]))
        s = c * n
        gx[s] = piece(x, 0, c, xp, gx_send.at[s], gx_recv.at[s])
        gc.append(piece(x, 0, c, sib, gc_send.at[s], gc_recv.at[s]))

    cxc.wait_recv()
    call[h, x] = (cx[:, x] + xc_in[...]).astype(BF16)
    col_x = remote(call.at[h, x], call.at[h, x], c_send.at[0], c_recv.at[0], xp)
    col_s = remote(call.at[h, x], call.at[h, x], c_send.at[1], c_recv.at[1], sib)
    col_x.start()
    col_s.start()
    sends += [col_x, col_s]

    for c in range(2):
        for d in range(1, n):
            s = c * n + d
            gz[c * (n - 1) + d - 1].wait_recv()
            gx[s] = piece(x, d, c, xp, gx_send.at[s], gx_recv.at[s])
            gc.append(piece(x, d, c, sib, gc_send.at[s], gc_recv.at[s]))
    col_x.wait_recv()
    other = call.at[h, 1 - x]
    col_f = remote(other, other, c_send.at[2], c_recv.at[2], sib)
    col_f.start()
    sends.append(col_f)
    for c in range(2):
        for d in range(n):
            s = c * n + d
            gx[s].wait_recv()
            gc.append(piece(1 - x, d, c, sib, gc_send.at[2 * n + s], gc_recv.at[2 * n + s]))

    col_s.wait_recv()
    col_f.wait_recv()
    for a in range(2):
        for b in range(2):
            col_out[:, b * BLK:(b + 1) * BLK, a * BLK:(a + 1) * BLK] = call[a, b]
    locs[3].wait()
    for c in gc:
        c.wait_recv()
    pr = dall.shape[4]
    for a in range(2):
        for b in range(2):
            for k in range(n):
                rs = slice(b * BLK + k * pr, b * BLK + (k + 1) * pr)
                cs = slice(a * BLK, (a + 1) * BLK)
                diag_out[:, rs, cs] = d_v[:, rs, cs] - dall[a, b, k]
    for c in sends:
        c.wait_send()


def fused(n, ainv, panel, upanel, dinv, pattern):
    w = ainv.shape[2]
    pr = BLK // n
    dma = pltpu.SemaphoreType.DMA
    hbm = pl.BlockSpec(memory_space=pltpu.HBM)
    vmem = pl.BlockSpec(memory_space=pltpu.VMEM)
    return pl.pallas_call(
        functools.partial(kernel, n),
        out_shape=(
            jax.ShapeDtypeStruct((2, w, w), BF16),
            jax.ShapeDtypeStruct((2, w, w), F32),
        ),
        in_specs=[hbm] * 5,
        out_specs=(vmem, vmem),
        scratch_shapes=[
            pltpu.SMEM((2, 2), jnp.int32),
            pltpu.VMEM((2, w, w), BF16),
            pltpu.VMEM((2, w, w), BF16),
            pltpu.VMEM((2, w, w), F32),
            pltpu.VMEM((2, w, w), BF16),
            pltpu.VMEM((2 * w, 2 * w), BF16),
            pltpu.VMEM((2 * w, 2 * w), BF16),
            pltpu.VMEM((2, 2 * w, BLK), F32),
            pltpu.VMEM((2 * w, BLK), F32),
            pltpu.VMEM((2, 2, BLK, BLK), F32),
            pltpu.VMEM((2, 2, n, pr, BLK), F32),
            pltpu.VMEM((2, n, pr, BLK), F32),
            pltpu.VMEM((2, BLK, BLK), F32),
            pltpu.VMEM((2, n, pr, BLK), F32),
            pltpu.VMEM((2, n, pr, BLK), F32),
            pltpu.VMEM((2, 2, n, 2, pr, BLK), F32),
            pltpu.VMEM((2, 2, 2, BLK, BLK), BF16),
            dma((5,)),
            dma((n,)), dma((n,)),
            dma, dma,
            dma((3,)), dma((3,)),
            dma((2 * n,)), dma((2 * n,)),
            dma((2 * n,)), dma((2 * n,)),
            dma((2 * n,)), dma((2 * n,)),
            dma((4 * n,)), dma((4 * n,)),
            dma((3,)), dma((3,)),
        ],
        compiler_params=pltpu.CompilerParams(
            collective_id=0, has_side_effects=True, vmem_limit_bytes=48 * 2**20),
        cost_estimate=pl.CostEstimate(
            flops=12 * w**3, bytes_accessed=12 * w * w, transcendentals=0),
    )(*(pltpu.with_memory_space_constraint(v, pltpu.HBM)
        for v in (ainv, panel, upanel, dinv, pattern)))


def complex_dot(left_re, left_im, right_re, right_im):
    real = jnp.dot(left_re, right_re, preferred_element_type=F32) - jnp.dot(
        left_im, right_im, preferred_element_type=F32
    )
    imag = jnp.dot(left_re, right_im, preferred_element_type=F32) + jnp.dot(
        left_im, right_re, preferred_element_type=F32
    )
    return (real, imag)


def upper_terms(up_full, column_full):
    hi = lax.Precision.HIGHEST
    d_re = jnp.dot(up_full[0], column_full[0], precision=hi) - jnp.dot(
        up_full[1], column_full[1], precision=hi
    )
    d_im = jnp.dot(up_full[0], column_full[1], precision=hi) + jnp.dot(
        up_full[1], column_full[0], precision=hi
    )
    return jnp.stack([d_re, d_im])


def general(ainv, panel, upanel, dinv, pattern):
    local_cols = ainv.shape[2]
    row_blocks = pattern.shape[0]
    col_blocks = pattern.shape[1]
    width = panel.shape[4]
    weights = pattern.astype(BF16)
    masked = (
        ainv.reshape(2, row_blocks, BLK, col_blocks, BLK) * weights[None, :, None, :, None]
    ).reshape(ainv.shape)
    gathered = lax.all_gather(panel, "prow", axis=2, tiled=True).reshape(2, local_cols, width)
    real, imag = complex_dot(masked[0], masked[1], gathered[0], gathered[1])
    column_full = lax.psum(jnp.stack([-real, -imag]), "pcol")
    column = column_full.astype(BF16)
    total = lax.psum(upper_terms(upanel.astype(F32), column_full), "prow")
    return (column, dinv - total)


def solution(mesh):
    n = mesh.shape["prow"]

    def per_device(ainv, panel, upanel, dinv, pattern):
        square = ainv.shape[1:] == (2 * BLK, 2 * BLK) and panel.shape[4] == 2 * BLK
        if n == 4 and mesh.shape["pcol"] == 4 and square:
            return fused(n, ainv, panel, upanel, dinv, pattern)
        return general(ainv, panel, upanel, dinv, pattern)

    in_specs = (
        P("pole", "prow", "pcol"),
        P("pole", "pcol", "prow", None, None),
        P("pole", None, "prow"),
        P("pole", None, None),
        P("prow", "pcol"),
    )
    out_specs = (P("pole", "prow", None), P("pole", None, None))
    return jax.shard_map(
        per_device, mesh=mesh, in_specs=in_specs, out_specs=out_specs, check_vma=False
    )
```

```python
import functools

import jax
import jax.numpy as jnp
from jax import lax
from jax.experimental import pallas as pl
from jax.experimental.pallas import tpu as pltpu
from jax.sharding import PartitionSpec as P

BLK = 128
MESH = pl.DeviceIdType.MESH
F32 = jnp.float32
BF16 = jnp.bfloat16


def kernel(n, ainv, panel, upanel, dinv, pattern, col_out, diag_out,
           pat_s, a_v, u_v, d_v, low, m_v, um_v, part, core_in, cx, xc_in, call,
           tbuf, d_in, s1, x_in, sbuf, z_in, dall,
           loc_sem, p_send, p_recv, b_send, b_recv, x_send, x_recv, z_send, z_recv,
           gz_send, gz_recv, gx_send, gx_recv, gc_send, gc_recv, c_send, c_recv):
    pole = lax.axis_index("pole")
    me = lax.axis_index("prow")
    j = lax.axis_index("pcol")
    h = lax.rem(j, 2)
    x = j // 2
    rows = panel.shape[3]
    z_peer = [lax.rem(me + d, n) for d in range(n)]
    z_from = [lax.rem(me + n - d, n) for d in range(n)]
    sib = (pole, me, j + 1 - 2 * h)
    xp = (pole, me, lax.rem(j + 2, 4))
    lanes = [slice(a * BLK, (a + 1) * BLK) for a in range(2)]

    def remote(src, dst, send, recv, device):
        return pltpu.make_async_remote_copy(
            src_ref=src, dst_ref=dst, send_sem=send, recv_sem=recv,
            device_id=device, device_id_type=MESH)

    my_rows = pl.ds(pl.multiple_of(me * rows, rows), rows)
    locs = [
        pltpu.make_async_copy(
            panel.at[:, 0, 0, :, lanes[0]], low.at[0, :, my_rows], loc_sem.at[0]),
        pltpu.make_async_copy(ainv, a_v, loc_sem.at[1]),
        pltpu.make_async_copy(upanel, u_v, loc_sem.at[2]),
        pltpu.make_async_copy(dinv, d_v, loc_sem.at[3]),
        pltpu.make_async_copy(pattern, pat_s, loc_sem.at[4]),
        pltpu.make_async_copy(
            panel.at[:, 0, 0, :, lanes[1]], low.at[1, :, my_rows], loc_sem.at[5]),
    ]
    for c in locs:
        c.start()
    barrier = pltpu.get_barrier_semaphore()
    others = [(pole, z_peer[d], j) for d in range(1, n)] + [sib, xp]
    for dev in others:
        pl.semaphore_signal(barrier, inc=1, device_id=dev, device_id_type=MESH)
    pl.semaphore_wait(barrier, len(others))

    sends = []
    gathers = [[], []]
    for a in range(2):
        for d in (2, 1, 3) if n == 4 else range(1, n):
            k = a * n + d
            c = remote(panel.at[:, 0, 0, :, lanes[a]], low.at[a, :, my_rows],
                       p_send.at[k], p_recv.at[k], (pole, z_peer[d], j))
            c.start()
            gathers[a].append(c)
            sends.append(c)

    locs[1].wait()
    locs[4].wait()
    w = a_v.shape[2]
    for bi in range(pattern.shape[0]):
        for bj in range(pattern.shape[1]):
            wt = pat_s[bi, bj].astype(F32)
            rs = slice(bi * BLK, (bi + 1) * BLK)
            cs = slice(bj * BLK, (bj + 1) * BLK)
            r0, c0 = bi * BLK, bj * BLK
            re = a_v[0, rs, cs].astype(F32) * wt
            im = a_v[1, rs, cs].astype(F32) * wt
            nre = (-re).astype(BF16)
            m_v[r0:r0 + BLK, c0:c0 + BLK] = nre
            m_v[w + r0:w + r0 + BLK, w + c0:w + c0 + BLK] = nre
            m_v[r0:r0 + BLK, w + c0:w + c0 + BLK] = im.astype(BF16)
            m_v[w + r0:w + r0 + BLK, c0:c0 + BLK] = (-im).astype(BF16)
    locs[2].wait()
    um_v[:w, :w] = u_v[0]
    um_v[w:, w:] = u_v[0]
    um_v[:w, w:] = -u_v[1]
    um_v[w:, :w] = u_v[1]

    def product(a):
        locs[(0, 5)[a]].wait()
        for c in gathers[a]:
            c.wait_recv()
        p = jnp.dot(m_v[...], low[a].reshape(2 * w, BLK), preferred_element_type=F32)
        part[a] = p
        hi = p.astype(BF16)
        lo = (p - hi.astype(F32)).astype(BF16)
        t = jnp.dot(um_v[...], jnp.concatenate([hi, lo], axis=1), preferred_element_type=F32)
        tbuf[a] = (t[:, :BLK] + t[:, BLK:]).reshape(tbuf.shape[1:])
        c = remote(tbuf.at[a, :, 1 - h], d_in.at[a], b_send.at[a], b_recv.at[a], sib)
        c.start()
        return c

    def over_core(a):
        dc[a].wait_recv()
        s1[a] = tbuf[a, :, h] + d_in[a]
        c = remote(s1.at[a, :, 1 - x], x_in.at[a], x_send.at[a], x_recv.at[a], xp)
        c.start()
        return c

    def over_x(a):
        dx[a].wait_recv()
        sbuf[a] = s1[a, :, x] + x_in[a]
        zs = []
        for d in range(1, n):
            k = a * n + d
            c = remote(sbuf.at[a, :, z_peer[d]], z_in.at[a, d], z_send.at[k],
                       z_recv.at[k], (pole, z_peer[d], j))
            c.start()
            zs.append(c)
        return zs

    def piece(side, d, a, dev, send, recv):
        slot = dall.at[h, side, z_from[d], a]
        c = remote(slot, slot, send, recv, dev)
        c.start()
        sends.append(c)
        return c

    gz, gx, gc = {}, {}, []

    def over_z(a):
        total = sbuf[a, :, me]
        for d in range(1, n):
            zs[a][d - 1].wait_recv()
            total = total + z_in[a, d]
        dall[h, x, me, a] = total
        for d in range(1, n):
            k = a * n + d
            gz[k] = piece(x, 0, a, (pole, z_peer[d], j), gz_send.at[k], gz_recv.at[k])
        k = a * n
        gx[k] = piece(x, 0, a, xp, gx_send.at[k], gx_recv.at[k])
        gc.append(piece(x, 0, a, sib, gc_send.at[k], gc_recv.at[k]))

    dc, dx, zs = [], [], []
    dc.append(product(0))
    dx.append(over_core(0))
    dc.append(product(1))
    cb = remote(part.at[1 - h], core_in, b_send.at[2], b_recv.at[2], sib)
    cb.start()
    zs.append(over_x(0))
    dx.append(over_core(1))
    cb.wait_recv()
    cx[...] = (part[h] + core_in[...]).reshape(cx.shape)
    cxc = remote(cx.at[:, 1 - x], xc_in, x_send.at[2], x_recv.at[2], xp)
    cxc.start()
    zs.append(over_x(1))
    sends += dc + dx + zs[0] + zs[1] + [cb, cxc]
    over_z(0)
    cxc.wait_recv()
    call[h, x] = (cx[:, x] + xc_in[...]).astype(BF16)
    col_x = remote(call.at[h, x], call.at[h, x], c_send.at[0], c_recv.at[0], xp)
    col_s = remote(call.at[h, x], call.at[h, x], c_send.at[1], c_recv.at[1], sib)
    col_x.start()
    col_s.start()
    sends += [col_x, col_s]
    over_z(1)
    for a in range(2):
        for d in range(1, n):
            k = a * n + d
            gz[k].wait_recv()
            gx[k] = piece(x, d, a, xp, gx_send.at[k], gx_recv.at[k])
            gc.append(piece(x, d, a, sib, gc_send.at[k], gc_recv.at[k]))
        if a == 0:
            col_x.wait_recv()
            other = call.at[h, 1 - x]
            col_f = remote(other, other, c_send.at[2], c_recv.at[2], sib)
            col_f.start()
            sends.append(col_f)
        for d in range(n):
            k = a * n + d
            gx[k].wait_recv()
            gc.append(piece(1 - x, d, a, sib, gc_send.at[2 * n + k], gc_recv.at[2 * n + k]))

    col_s.wait_recv()
    col_f.wait_recv()
    for a in range(2):
        for b in range(2):
            col_out[:, b * BLK:(b + 1) * BLK, lanes[a]] = call[a, b]
    locs[3].wait()
    for c in gc:
        c.wait_recv()
    pr = dall.shape[5]
    for g in range(2):
        for b in range(2):
            for k in range(n):
                r0 = g * BLK + (b * n + k) * pr
                for a in range(2):
                    diag_out[:, r0:r0 + pr, lanes[a]] = (
                        d_v[:, r0:r0 + pr, lanes[a]] - dall[g, b, k, a])
    for c in sends:
        c.wait_send()


def fused(n, ainv, panel, upanel, dinv, pattern):
    w = ainv.shape[2]
    pr = BLK // 2 // n
    dma = pltpu.SemaphoreType.DMA
    hbm = pl.BlockSpec(memory_space=pltpu.HBM)
    vmem = pl.BlockSpec(memory_space=pltpu.VMEM)
    return pl.pallas_call(
        functools.partial(kernel, n),
        out_shape=(
            jax.ShapeDtypeStruct((2, w, w), BF16),
            jax.ShapeDtypeStruct((2, w, w), F32),
        ),
        in_specs=[hbm] * 5,
        out_specs=(vmem, vmem),
        scratch_shapes=[
            pltpu.SMEM((2, 2), jnp.int32),
            pltpu.VMEM((2, w, w), BF16),
            pltpu.VMEM((2, w, w), BF16),
            pltpu.VMEM((2, w, w), F32),
            pltpu.VMEM((2, 2, w, BLK), BF16),
            pltpu.VMEM((2 * w, 2 * w), BF16),
            pltpu.VMEM((2 * w, 2 * w), BF16),
            pltpu.VMEM((2, 2 * w, BLK), F32),
            pltpu.VMEM((2 * w, BLK), F32),
            pltpu.VMEM((2, 2, BLK, BLK), F32),
            pltpu.VMEM((2, BLK, BLK), F32),
            pltpu.VMEM((2, 2, 2, BLK, BLK), BF16),
            pltpu.VMEM((2, 2, 2, 2, n, pr, BLK), F32),
            pltpu.VMEM((2, 2, 2, n, pr, BLK), F32),
            pltpu.VMEM((2, 2, 2, n, pr, BLK), F32),
            pltpu.VMEM((2, 2, n, pr, BLK), F32),
            pltpu.VMEM((2, 2, n, pr, BLK), F32),
            pltpu.VMEM((2, n, 2, pr, BLK), F32),
            pltpu.VMEM((2, 2, n, 2, 2, pr, BLK), F32),
            dma((6,)),
            dma((2 * n,)), dma((2 * n,)),
            dma((3,)), dma((3,)),
            dma((3,)), dma((3,)),
            dma((2 * n,)), dma((2 * n,)),
            dma((2 * n,)), dma((2 * n,)),
            dma((2 * n,)), dma((2 * n,)),
            dma((4 * n,)), dma((4 * n,)),
            dma((3,)), dma((3,)),
        ],
        compiler_params=pltpu.CompilerParams(
            collective_id=0, has_side_effects=True, vmem_limit_bytes=48 * 2**20),
        cost_estimate=pl.CostEstimate(
            flops=12 * w**3, bytes_accessed=12 * w * w, transcendentals=0),
    )(*(pltpu.with_memory_space_constraint(v, pltpu.HBM)
        for v in (ainv, panel, upanel, dinv, pattern)))


def complex_dot(left_re, left_im, right_re, right_im):
    real = jnp.dot(left_re, right_re, preferred_element_type=F32) - jnp.dot(
        left_im, right_im, preferred_element_type=F32
    )
    imag = jnp.dot(left_re, right_im, preferred_element_type=F32) + jnp.dot(
        left_im, right_re, preferred_element_type=F32
    )
    return (real, imag)


def upper_terms(up_full, column_full):
    hi = lax.Precision.HIGHEST
    d_re = jnp.dot(up_full[0], column_full[0], precision=hi) - jnp.dot(
        up_full[1], column_full[1], precision=hi
    )
    d_im = jnp.dot(up_full[0], column_full[1], precision=hi) + jnp.dot(
        up_full[1], column_full[0], precision=hi
    )
    return jnp.stack([d_re, d_im])


def general(ainv, panel, upanel, dinv, pattern):
    local_cols = ainv.shape[2]
    row_blocks = pattern.shape[0]
    col_blocks = pattern.shape[1]
    width = panel.shape[4]
    weights = pattern.astype(BF16)
    masked = (
        ainv.reshape(2, row_blocks, BLK, col_blocks, BLK) * weights[None, :, None, :, None]
    ).reshape(ainv.shape)
    gathered = lax.all_gather(panel, "prow", axis=2, tiled=True).reshape(2, local_cols, width)
    real, imag = complex_dot(masked[0], masked[1], gathered[0], gathered[1])
    column_full = lax.psum(jnp.stack([-real, -imag]), "pcol")
    column = column_full.astype(BF16)
    total = lax.psum(upper_terms(upanel.astype(F32), column_full), "prow")
    return (column, dinv - total)


def solution(mesh):
    n = mesh.shape["prow"]

    def per_device(ainv, panel, upanel, dinv, pattern):
        square = ainv.shape[1:] == (2 * BLK, 2 * BLK) and panel.shape[4] == 2 * BLK
        if n == 4 and mesh.shape["pcol"] == 4 and square:
            return fused(n, ainv, panel, upanel, dinv, pattern)
        return general(ainv, panel, upanel, dinv, pattern)

    in_specs = (
        P("pole", "prow", "pcol"),
        P("pole", "pcol", "prow", None, None),
        P("pole", None, "prow"),
        P("pole", None, None),
        P("prow", "pcol"),
    )
    out_specs = (P("pole", "prow", None), P("pole", None, None))
    return jax.shard_map(
        per_device, mesh=mesh, in_specs=in_specs, out_specs=out_specs, check_vma=False
    )
```

```python
import functools

import jax
import jax.numpy as jnp
from jax import lax
from jax.experimental import pallas as pl
from jax.experimental.pallas import tpu as pltpu
from jax.sharding import PartitionSpec as P

BLK = 128
MESH = pl.DeviceIdType.MESH
F32 = jnp.float32
BF16 = jnp.bfloat16


def kernel(n, ainv, panel, upanel, dinv, pattern, col_out, diag_out,
           pat_s, a_v, u_v, d_v, low, m_v, um_v, part, core_in, cx, tbuf, xc_in,
           r_in, dall, call,
           loc_sem, p_send, p_recv, b_send, b_recv, x_send, x_recv, r_send, r_recv,
           g_send, g_recv, gc_send, gc_recv, c_send, c_recv):
    pole = lax.axis_index("pole")
    me = lax.axis_index("prow")
    j = lax.axis_index("pcol")
    h = lax.rem(j, 2)
    x = j // 2
    rows = panel.shape[3]
    z_peer = [lax.rem(me + d, n) for d in range(n)]
    z_from = [lax.rem(me + n - d, n) for d in range(n)]
    sib = (pole, me, j + 1 - 2 * h)
    xp = (pole, me, lax.rem(j + 2, 4))
    hops = [(f, d) for d in (2, 3, 1, 0) for f in (1, 0) if (f, d) != (0, 0)]
    spot = [(lax.rem(x + f, 2), z_peer[d]) for f, d in hops]
    seven = [(pole, zz, 2 * xx + h) for xx, zz in spot]

    def remote(src, dst, send, recv, device):
        return pltpu.make_async_remote_copy(
            src_ref=src, dst_ref=dst, send_sem=send, recv_sem=recv,
            device_id=device, device_id_type=MESH)

    my_rows = pl.ds(pl.multiple_of(me * rows, rows), rows)
    locs = [
        pltpu.make_async_copy(panel.at[:, 0, 0], low.at[:, my_rows], loc_sem.at[0]),
        pltpu.make_async_copy(ainv, a_v, loc_sem.at[1]),
        pltpu.make_async_copy(upanel, u_v, loc_sem.at[2]),
        pltpu.make_async_copy(dinv, d_v, loc_sem.at[3]),
        pltpu.make_async_copy(pattern, pat_s, loc_sem.at[4]),
    ]
    for c in locs:
        c.start()
    barrier = pltpu.get_barrier_semaphore()
    others = seven + [sib]
    for dev in others:
        pl.semaphore_signal(barrier, inc=1, device_id=dev, device_id_type=MESH)
    pl.semaphore_wait(barrier, len(others))

    sends = []
    gathers = []
    for d in range(1, n):
        c = remote(panel.at[:, 0, 0], low.at[:, my_rows], p_send.at[d], p_recv.at[d],
                   (pole, z_peer[d], j))
        c.start()
        gathers.append(c)
        sends.append(c)

    locs[1].wait()
    locs[4].wait()
    w = a_v.shape[2]
    for bi in range(pattern.shape[0]):
        for bj in range(pattern.shape[1]):
            wt = pat_s[bi, bj].astype(F32)
            rs = slice(bi * BLK, (bi + 1) * BLK)
            cs = slice(bj * BLK, (bj + 1) * BLK)
            r0, c0 = bi * BLK, bj * BLK
            re = a_v[0, rs, cs].astype(F32) * wt
            im = a_v[1, rs, cs].astype(F32) * wt
            nre = (-re).astype(BF16)
            m_v[r0:r0 + BLK, c0:c0 + BLK] = nre
            m_v[w + r0:w + r0 + BLK, w + c0:w + c0 + BLK] = nre
            m_v[r0:r0 + BLK, w + c0:w + c0 + BLK] = im.astype(BF16)
            m_v[w + r0:w + r0 + BLK, c0:c0 + BLK] = (-im).astype(BF16)
    locs[2].wait()
    um_v[:w, :w] = u_v[0]
    um_v[w:, w:] = u_v[0]
    um_v[:w, w:] = -u_v[1]
    um_v[w:, :w] = u_v[1]
    locs[0].wait()
    for c in gathers:
        c.wait_recv()

    prod = jnp.dot(m_v[...], low[...].reshape(2 * w, w), preferred_element_type=F32)
    part[0] = prod[:, :BLK]
    part[1] = prod[:, BLK:]
    c = remote(part.at[1 - h], core_in, b_send, b_recv, sib)
    c.start()
    c.wait_recv()
    sends.append(c)

    half = part[h] + core_in[...]
    cx[...] = half.reshape(cx.shape)
    hi = half.astype(BF16)
    lo = (half - hi.astype(F32)).astype(BF16)
    t = jnp.dot(um_v[...], jnp.concatenate([hi, lo], axis=1), preferred_element_type=F32)
    tbuf[...] = (t[:, :BLK] + t[:, BLK:]).reshape(tbuf.shape)
    k7 = len(hops)
    rs = []
    for c in range(2):
        for i, (xx, zz) in enumerate(spot):
            s = c * k7 + i
            rs.append(remote(tbuf.at[c, xx, zz], r_in.at[s], r_send.at[s], r_recv.at[s],
                             seven[i]))
            rs[s].start()
    cxc = remote(cx.at[:, 1 - x], xc_in, x_send, x_recv, xp)
    cxc.start()
    sends += rs + [cxc]

    ag = []
    for c in range(2):
        total = tbuf[c, x, me]
        for i in range(k7):
            rs[c * k7 + i].wait_recv()
            total = total + r_in[c * k7 + i]
        dall[h, c, x, me] = total
        mine = dall.at[h, c, x, me]
        for i in range(k7):
            s = c * k7 + i
            ag.append(remote(mine, mine, g_send.at[s], g_recv.at[s], seven[i]))
            ag[s].start()
    sends += ag

    cxc.wait_recv()
    call[h, x] = (cx[:, x] + xc_in[...]).astype(BF16)
    col_x = remote(call.at[h, x], call.at[h, x], c_send.at[0], c_recv.at[0], xp)
    col_s = remote(call.at[h, x], call.at[h, x], c_send.at[1], c_recv.at[1], sib)
    col_x.start()
    col_s.start()
    sends += [col_x, col_s]
    col_x.wait_recv()
    other = call.at[h, 1 - x]
    col_f = remote(other, other, c_send.at[2], c_recv.at[2], sib)
    col_f.start()
    sends.append(col_f)

    gc = []
    for c in range(2):
        for i in range(k7):
            ag[c * k7 + i].wait_recv()
        gc.append(remote(dall.at[h, c], dall.at[h, c], gc_send.at[c], gc_recv.at[c], sib))
        gc[c].start()
    sends += gc

    col_s.wait_recv()
    col_f.wait_recv()
    for a in range(2):
        for b in range(2):
            col_out[:, b * BLK:(b + 1) * BLK, a * BLK:(a + 1) * BLK] = call[a, b]
    locs[3].wait()
    pr = dall.shape[4]
    for c in range(2):
        gc[c].wait_recv()
        for a in range(2):
            for b in range(2):
                rs = slice(b * BLK, (b + 1) * BLK)
                cs = slice(a * BLK, (a + 1) * BLK)
                diag_out[c, rs, cs] = d_v[c, rs, cs] - dall[a, c, b].reshape(n * pr, BLK)
    for c in sends:
        c.wait_send()


def fused(n, ainv, panel, upanel, dinv, pattern):
    w = ainv.shape[2]
    pr = BLK // n
    dma = pltpu.SemaphoreType.DMA
    hbm = pl.BlockSpec(memory_space=pltpu.HBM)
    vmem = pl.BlockSpec(memory_space=pltpu.VMEM)
    return pl.pallas_call(
        functools.partial(kernel, n),
        out_shape=(
            jax.ShapeDtypeStruct((2, w, w), BF16),
            jax.ShapeDtypeStruct((2, w, w), F32),
        ),
        in_specs=[hbm] * 5,
        out_specs=(vmem, vmem),
        scratch_shapes=[
            pltpu.SMEM((2, 2), jnp.int32),
            pltpu.VMEM((2, w, w), BF16),
            pltpu.VMEM((2, w, w), BF16),
            pltpu.VMEM((2, w, w), F32),
            pltpu.VMEM((2, w, w), BF16),
            pltpu.VMEM((2 * w, 2 * w), BF16),
            pltpu.VMEM((2 * w, 2 * w), BF16),
            pltpu.VMEM((2, 2 * w, BLK), F32),
            pltpu.VMEM((2 * w, BLK), F32),
            pltpu.VMEM((2, 2, BLK, BLK), F32),
            pltpu.VMEM((2, 2, n, pr, BLK), F32),
            pltpu.VMEM((2, BLK, BLK), F32),
            pltpu.VMEM((4 * n - 2, pr, BLK), F32),
            pltpu.VMEM((2, 2, 2, n, pr, BLK), F32),
            pltpu.VMEM((2, 2, 2, BLK, BLK), BF16),
            dma((5,)),
            dma((n,)), dma((n,)),
            dma, dma,
            dma, dma,
            dma((4 * n - 2,)), dma((4 * n - 2,)),
            dma((4 * n - 2,)), dma((4 * n - 2,)),
            dma((2,)), dma((2,)),
            dma((3,)), dma((3,)),
        ],
        compiler_params=pltpu.CompilerParams(
            collective_id=0, has_side_effects=True, vmem_limit_bytes=48 * 2**20),
        cost_estimate=pl.CostEstimate(
            flops=12 * w**3, bytes_accessed=12 * w * w, transcendentals=0),
    )(*(pltpu.with_memory_space_constraint(v, pltpu.HBM)
        for v in (ainv, panel, upanel, dinv, pattern)))


def complex_dot(left_re, left_im, right_re, right_im):
    real = jnp.dot(left_re, right_re, preferred_element_type=F32) - jnp.dot(
        left_im, right_im, preferred_element_type=F32
    )
    imag = jnp.dot(left_re, right_im, preferred_element_type=F32) + jnp.dot(
        left_im, right_re, preferred_element_type=F32
    )
    return (real, imag)


def upper_terms(up_full, column_full):
    hi = lax.Precision.HIGHEST
    d_re = jnp.dot(up_full[0], column_full[0], precision=hi) - jnp.dot(
        up_full[1], column_full[1], precision=hi
    )
    d_im = jnp.dot(up_full[0], column_full[1], precision=hi) + jnp.dot(
        up_full[1], column_full[0], precision=hi
    )
    return jnp.stack([d_re, d_im])


def general(ainv, panel, upanel, dinv, pattern):
    local_cols = ainv.shape[2]
    row_blocks = pattern.shape[0]
    col_blocks = pattern.shape[1]
    width = panel.shape[4]
    weights = pattern.astype(BF16)
    masked = (
        ainv.reshape(2, row_blocks, BLK, col_blocks, BLK) * weights[None, :, None, :, None]
    ).reshape(ainv.shape)
    gathered = lax.all_gather(panel, "prow", axis=2, tiled=True).reshape(2, local_cols, width)
    real, imag = complex_dot(masked[0], masked[1], gathered[0], gathered[1])
    column_full = lax.psum(jnp.stack([-real, -imag]), "pcol")
    column = column_full.astype(BF16)
    total = lax.psum(upper_terms(upanel.astype(F32), column_full), "prow")
    return (column, dinv - total)


def solution(mesh):
    n = mesh.shape["prow"]

    def per_device(ainv, panel, upanel, dinv, pattern):
        square = ainv.shape[1:] == (2 * BLK, 2 * BLK) and panel.shape[4] == 2 * BLK
        if n == 4 and mesh.shape["pcol"] == 4 and square:
            return fused(n, ainv, panel, upanel, dinv, pattern)
        return general(ainv, panel, upanel, dinv, pattern)

    in_specs = (
        P("pole", "prow", "pcol"),
        P("pole", "pcol", "prow", None, None),
        P("pole", None, "prow"),
        P("pole", None, None),
        P("prow", "pcol"),
    )
    out_specs = (P("pole", "prow", None), P("pole", None, None))
    return jax.shard_map(
        per_device, mesh=mesh, in_specs=in_specs, out_specs=out_specs, check_vma=False
    )
```

```python
import functools

import jax
import jax.numpy as jnp
from jax import lax
from jax.experimental import pallas as pl
from jax.experimental.pallas import tpu as pltpu
from jax.sharding import PartitionSpec as P

BLK = 128
MESH = pl.DeviceIdType.MESH
F32 = jnp.float32
BF16 = jnp.bfloat16


def kernel(n, ainv, panel, upanel, dinv, pattern, col_out, diag_out,
           pat_s, a_v, u_v, d_v, low, m_v, um_v, part, core_in, cx, tbuf, xc_in,
           r_in, dall, call,
           loc_sem, p_send, p_recv, b_send, b_recv, x_send, x_recv, r_send, r_recv,
           g_send, g_recv, gc_send, gc_recv, c_send, c_recv):
    pole = lax.axis_index("pole")
    me = lax.axis_index("prow")
    j = lax.axis_index("pcol")
    h = lax.rem(j, 2)
    x = j // 2
    rows = panel.shape[3]
    z_peer = [lax.rem(me + d, n) for d in range(n)]
    z_from = [lax.rem(me + n - d, n) for d in range(n)]
    sib = (pole, me, j + 1 - 2 * h)
    xp = (pole, me, lax.rem(j + 2, 4))
    hops = [(f, d) for d in (2, 3, 1, 0) for f in (1, 0) if (f, d) != (0, 0)]
    spot = [(lax.rem(x + f, 2), z_peer[d]) for f, d in hops]
    seven = [(pole, zz, 2 * xx + h) for xx, zz in spot]

    def remote(src, dst, send, recv, device):
        return pltpu.make_async_remote_copy(
            src_ref=src, dst_ref=dst, send_sem=send, recv_sem=recv,
            device_id=device, device_id_type=MESH)

    my_rows = pl.ds(pl.multiple_of(me * rows, rows), rows)
    locs = [
        pltpu.make_async_copy(panel.at[:, 0, 0], low.at[:, my_rows], loc_sem.at[0]),
        pltpu.make_async_copy(ainv, a_v, loc_sem.at[1]),
        pltpu.make_async_copy(upanel, u_v, loc_sem.at[2]),
        pltpu.make_async_copy(dinv, d_v, loc_sem.at[3]),
        pltpu.make_async_copy(pattern, pat_s, loc_sem.at[4]),
    ]
    for c in locs:
        c.start()
    barrier = pltpu.get_barrier_semaphore()
    others = seven + [sib]
    for dev in others:
        pl.semaphore_signal(barrier, inc=1, device_id=dev, device_id_type=MESH)
    pl.semaphore_wait(barrier, len(others))

    sends = []
    gathers = []
    for d in (2, 1, 3):
        c = remote(panel.at[:, 0, 0], low.at[:, my_rows], p_send.at[d], p_recv.at[d],
                   (pole, z_peer[d], j))
        c.start()
        gathers.append(c)
        sends.append(c)

    locs[1].wait()
    locs[4].wait()
    w = a_v.shape[2]
    for bi in range(pattern.shape[0]):
        for bj in range(pattern.shape[1]):
            wt = pat_s[bi, bj].astype(F32)
            rs = slice(bi * BLK, (bi + 1) * BLK)
            cs = slice(bj * BLK, (bj + 1) * BLK)
            r0, c0 = bi * BLK, bj * BLK
            re = a_v[0, rs, cs].astype(F32) * wt
            im = a_v[1, rs, cs].astype(F32) * wt
            nre = (-re).astype(BF16)
            m_v[r0:r0 + BLK, c0:c0 + BLK] = nre
            m_v[w + r0:w + r0 + BLK, w + c0:w + c0 + BLK] = nre
            m_v[r0:r0 + BLK, w + c0:w + c0 + BLK] = im.astype(BF16)
            m_v[w + r0:w + r0 + BLK, c0:c0 + BLK] = (-im).astype(BF16)
    locs[2].wait()
    um_v[:w, :w] = u_v[0]
    um_v[w:, w:] = u_v[0]
    um_v[:w, w:] = -u_v[1]
    um_v[w:, :w] = u_v[1]
    locs[0].wait()
    for c in gathers:
        c.wait_recv()

    full = low[...].reshape(2 * w, w)
    swap = []
    for c in range(2):
        rs = slice(c * w, (c + 1) * w)
        prod = jnp.dot(m_v[rs, :], full, preferred_element_type=F32)
        part[0, rs] = prod[:, :BLK]
        part[1, rs] = prod[:, BLK:]
        swap.append(remote(part.at[1 - h, rs], core_in.at[rs], b_send.at[c], b_recv.at[c], sib))
        swap[c].start()
    for c in swap:
        c.wait_recv()
    sends += swap

    half = part[h] + core_in[...]
    cx[...] = half.reshape(cx.shape)
    hi = half.astype(BF16)
    lo = (half - hi.astype(F32)).astype(BF16)
    t = jnp.dot(um_v[...], jnp.concatenate([hi, lo], axis=1), preferred_element_type=F32)
    tbuf[...] = (t[:, :BLK] + t[:, BLK:]).reshape(tbuf.shape)
    k7 = len(hops)
    rs = []
    for c in range(2):
        for i, (xx, zz) in enumerate(spot):
            s = c * k7 + i
            rs.append(remote(tbuf.at[c, xx, zz], r_in.at[s], r_send.at[s], r_recv.at[s],
                             seven[i]))
            rs[s].start()
    cxc = remote(cx.at[:, 1 - x], xc_in, x_send, x_recv, xp)
    cxc.start()
    sends += rs + [cxc]

    ag = []
    for c in range(2):
        total = tbuf[c, x, me]
        for i in range(k7):
            rs[c * k7 + i].wait_recv()
            total = total + r_in[c * k7 + i]
        dall[h, c, x, me] = total
        mine = dall.at[h, c, x, me]
        for i in range(k7):
            s = c * k7 + i
            ag.append(remote(mine, mine, g_send.at[s], g_recv.at[s], seven[i]))
            ag[s].start()
    sends += ag

    cxc.wait_recv()
    call[h, x] = (cx[:, x] + xc_in[...]).astype(BF16)
    col_x = remote(call.at[h, x], call.at[h, x], c_send.at[0], c_recv.at[0], xp)
    col_s = remote(call.at[h, x], call.at[h, x], c_send.at[1], c_recv.at[1], sib)
    col_x.start()
    col_s.start()
    sends += [col_x, col_s]
    col_x.wait_recv()
    other = call.at[h, 1 - x]
    col_f = remote(other, other, c_send.at[2], c_recv.at[2], sib)
    col_f.start()
    sends.append(col_f)

    gc = []
    for c in range(2):
        for i in range(k7):
            ag[c * k7 + i].wait_recv()
        gc.append(remote(dall.at[h, c], dall.at[h, c], gc_send.at[c], gc_recv.at[c], sib))
        gc[c].start()
    sends += gc

    col_s.wait_recv()
    col_f.wait_recv()
    for a in range(2):
        for b in range(2):
            col_out[:, b * BLK:(b + 1) * BLK, a * BLK:(a + 1) * BLK] = call[a, b]
    locs[3].wait()
    pr = dall.shape[4]
    for c in range(2):
        gc[c].wait_recv()
        for a in range(2):
            for b in range(2):
                rs = slice(b * BLK, (b + 1) * BLK)
                cs = slice(a * BLK, (a + 1) * BLK)
                diag_out[c, rs, cs] = d_v[c, rs, cs] - dall[a, c, b].reshape(n * pr, BLK)
    for c in sends:
        c.wait_send()


def fused(n, ainv, panel, upanel, dinv, pattern):
    w = ainv.shape[2]
    pr = BLK // n
    dma = pltpu.SemaphoreType.DMA
    hbm = pl.BlockSpec(memory_space=pltpu.HBM)
    vmem = pl.BlockSpec(memory_space=pltpu.VMEM)
    return pl.pallas_call(
        functools.partial(kernel, n),
        out_shape=(
            jax.ShapeDtypeStruct((2, w, w), BF16),
            jax.ShapeDtypeStruct((2, w, w), F32),
        ),
        in_specs=[hbm] * 5,
        out_specs=(vmem, vmem),
        scratch_shapes=[
            pltpu.SMEM((2, 2), jnp.int32),
            pltpu.VMEM((2, w, w), BF16),
            pltpu.VMEM((2, w, w), BF16),
            pltpu.VMEM((2, w, w), F32),
            pltpu.VMEM((2, w, w), BF16),
            pltpu.VMEM((2 * w, 2 * w), BF16),
            pltpu.VMEM((2 * w, 2 * w), BF16),
            pltpu.VMEM((2, 2 * w, BLK), F32),
            pltpu.VMEM((2 * w, BLK), F32),
            pltpu.VMEM((2, 2, BLK, BLK), F32),
            pltpu.VMEM((2, 2, n, pr, BLK), F32),
            pltpu.VMEM((2, BLK, BLK), F32),
            pltpu.VMEM((4 * n - 2, pr, BLK), F32),
            pltpu.VMEM((2, 2, 2, n, pr, BLK), F32),
            pltpu.VMEM((2, 2, 2, BLK, BLK), BF16),
            dma((5,)),
            dma((n,)), dma((n,)),
            dma((2,)), dma((2,)),
            dma, dma,
            dma((4 * n - 2,)), dma((4 * n - 2,)),
            dma((4 * n - 2,)), dma((4 * n - 2,)),
            dma((2,)), dma((2,)),
            dma((3,)), dma((3,)),
        ],
        compiler_params=pltpu.CompilerParams(
            collective_id=0, has_side_effects=True, vmem_limit_bytes=48 * 2**20),
        cost_estimate=pl.CostEstimate(
            flops=12 * w**3, bytes_accessed=12 * w * w, transcendentals=0),
    )(*(pltpu.with_memory_space_constraint(v, pltpu.HBM)
        for v in (ainv, panel, upanel, dinv, pattern)))


def complex_dot(left_re, left_im, right_re, right_im):
    real = jnp.dot(left_re, right_re, preferred_element_type=F32) - jnp.dot(
        left_im, right_im, preferred_element_type=F32
    )
    imag = jnp.dot(left_re, right_im, preferred_element_type=F32) + jnp.dot(
        left_im, right_re, preferred_element_type=F32
    )
    return (real, imag)


def upper_terms(up_full, column_full):
    hi = lax.Precision.HIGHEST
    d_re = jnp.dot(up_full[0], column_full[0], precision=hi) - jnp.dot(
        up_full[1], column_full[1], precision=hi
    )
    d_im = jnp.dot(up_full[0], column_full[1], precision=hi) + jnp.dot(
        up_full[1], column_full[0], precision=hi
    )
    return jnp.stack([d_re, d_im])


def general(ainv, panel, upanel, dinv, pattern):
    local_cols = ainv.shape[2]
    row_blocks = pattern.shape[0]
    col_blocks = pattern.shape[1]
    width = panel.shape[4]
    weights = pattern.astype(BF16)
    masked = (
        ainv.reshape(2, row_blocks, BLK, col_blocks, BLK) * weights[None, :, None, :, None]
    ).reshape(ainv.shape)
    gathered = lax.all_gather(panel, "prow", axis=2, tiled=True).reshape(2, local_cols, width)
    real, imag = complex_dot(masked[0], masked[1], gathered[0], gathered[1])
    column_full = lax.psum(jnp.stack([-real, -imag]), "pcol")
    column = column_full.astype(BF16)
    total = lax.psum(upper_terms(upanel.astype(F32), column_full), "prow")
    return (column, dinv - total)


def solution(mesh):
    n = mesh.shape["prow"]

    def per_device(ainv, panel, upanel, dinv, pattern):
        square = ainv.shape[1:] == (2 * BLK, 2 * BLK) and panel.shape[4] == 2 * BLK
        if n == 4 and mesh.shape["pcol"] == 4 and square:
            return fused(n, ainv, panel, upanel, dinv, pattern)
        return general(ainv, panel, upanel, dinv, pattern)

    in_specs = (
        P("pole", "prow", "pcol"),
        P("pole", "pcol", "prow", None, None),
        P("pole", None, "prow"),
        P("pole", None, None),
        P("prow", "pcol"),
    )
    out_specs = (P("pole", "prow", None), P("pole", None, None))
    return jax.shard_map(
        per_device, mesh=mesh, in_specs=in_specs, out_specs=out_specs, check_vma=False
    )
```

```python
import functools

import jax
import jax.numpy as jnp
from jax import lax
from jax.experimental import pallas as pl
from jax.experimental.pallas import tpu as pltpu
from jax.sharding import PartitionSpec as P

BLK = 128
MESH = pl.DeviceIdType.MESH
F32 = jnp.float32
BF16 = jnp.bfloat16


def kernel(n, ainv, panel, upanel, dinv, pattern, col_out, diag_out,
           pat_s, a_v, u_v, d_v, low, m_v, um_v, part, core_in, cx, tbuf, xc_in,
           r_in, dall, call,
           loc_sem, p_send, p_recv, b_send, b_recv, x_send, x_recv, r_send, r_recv,
           g_send, g_recv, gc_send, gc_recv, c_send, c_recv):
    pole = lax.axis_index("pole")
    me = lax.axis_index("prow")
    j = lax.axis_index("pcol")
    h = lax.rem(j, 2)
    x = j // 2
    rows = panel.shape[3]
    z_peer = [lax.rem(me + d, n) for d in range(n)]
    z_from = [lax.rem(me + n - d, n) for d in range(n)]
    sib = (pole, me, j + 1 - 2 * h)
    xp = (pole, me, lax.rem(j + 2, 4))
    hops = [(f, d) for f in (1, 0) for d in (2, 1, 3, 0) if (f, d) != (0, 0)]
    spot = [(lax.rem(x + f, 2), z_peer[d]) for f, d in hops]
    seven = [(pole, zz, 2 * xx + h) for xx, zz in spot]

    def remote(src, dst, send, recv, device):
        return pltpu.make_async_remote_copy(
            src_ref=src, dst_ref=dst, send_sem=send, recv_sem=recv,
            device_id=device, device_id_type=MESH)

    my_rows = pl.ds(pl.multiple_of(me * rows, rows), rows)
    locs = [
        pltpu.make_async_copy(panel.at[:, 0, 0], low.at[:, my_rows], loc_sem.at[0]),
        pltpu.make_async_copy(ainv, a_v, loc_sem.at[1]),
        pltpu.make_async_copy(upanel, u_v, loc_sem.at[2]),
        pltpu.make_async_copy(dinv, d_v, loc_sem.at[3]),
        pltpu.make_async_copy(pattern, pat_s, loc_sem.at[4]),
    ]
    for c in locs:
        c.start()
    barrier = pltpu.get_barrier_semaphore()
    others = seven + [sib]
    for dev in others:
        pl.semaphore_signal(barrier, inc=1, device_id=dev, device_id_type=MESH)
    pl.semaphore_wait(barrier, len(others))

    sends = []
    gathers = []
    for d in (2, 1, 3):
        c = remote(panel.at[:, 0, 0], low.at[:, my_rows], p_send.at[d], p_recv.at[d],
                   (pole, z_peer[d], j))
        c.start()
        gathers.append(c)
        sends.append(c)

    locs[1].wait()
    locs[4].wait()
    w = a_v.shape[2]
    for bi in range(pattern.shape[0]):
        for bj in range(pattern.shape[1]):
            wt = pat_s[bi, bj].astype(F32)
            rs = slice(bi * BLK, (bi + 1) * BLK)
            cs = slice(bj * BLK, (bj + 1) * BLK)
            r0, c0 = bi * BLK, bj * BLK
            re = a_v[0, rs, cs].astype(F32) * wt
            im = a_v[1, rs, cs].astype(F32) * wt
            nre = (-re).astype(BF16)
            m_v[r0:r0 + BLK, c0:c0 + BLK] = nre
            m_v[w + r0:w + r0 + BLK, w + c0:w + c0 + BLK] = nre
            m_v[r0:r0 + BLK, w + c0:w + c0 + BLK] = im.astype(BF16)
            m_v[w + r0:w + r0 + BLK, c0:c0 + BLK] = (-im).astype(BF16)
    locs[2].wait()
    um_v[:w, :w] = u_v[0]
    um_v[w:, w:] = u_v[0]
    um_v[:w, w:] = -u_v[1]
    um_v[w:, :w] = u_v[1]
    locs[0].wait()
    for c in gathers:
        c.wait_recv()

    full = low[...].reshape(2 * w, w)
    swap = []
    for c in range(2):
        rs = slice(c * w, (c + 1) * w)
        prod = jnp.dot(m_v[rs, :], full, preferred_element_type=F32)
        part[0, rs] = prod[:, :BLK]
        part[1, rs] = prod[:, BLK:]
        swap.append(remote(part.at[1 - h, rs], core_in.at[rs], b_send.at[c], b_recv.at[c], sib))
        swap[c].start()
    for c in swap:
        c.wait_recv()
    sends += swap

    half = part[h] + core_in[...]
    cx[...] = half.reshape(cx.shape)
    hi = half.astype(BF16)
    lo = (half - hi.astype(F32)).astype(BF16)
    t = jnp.dot(um_v[...], jnp.concatenate([hi, lo], axis=1), preferred_element_type=F32)
    tbuf[...] = (t[:, :BLK] + t[:, BLK:]).reshape(tbuf.shape)
    k7 = len(hops)
    rs = []
    for c in range(2):
        for i, (xx, zz) in enumerate(spot):
            s = c * k7 + i
            rs.append(remote(tbuf.at[c, xx, zz], r_in.at[s], r_send.at[s], r_recv.at[s],
                             seven[i]))
            rs[s].start()
    cxc = remote(cx.at[:, 1 - x], xc_in, x_send, x_recv, xp)
    cxc.start()
    sends += rs + [cxc]

    ag = []
    for c in range(2):
        total = tbuf[c, x, me]
        for i in range(k7):
            rs[c * k7 + i].wait_recv()
            total = total + r_in[c * k7 + i]
        dall[h, c, x, me] = total
        mine = dall.at[h, c, x, me]
        for i in range(k7):
            s = c * k7 + i
            ag.append(remote(mine, mine, g_send.at[s], g_recv.at[s], seven[i]))
            ag[s].start()
    sends += ag

    cxc.wait_recv()
    call[h, x] = (cx[:, x] + xc_in[...]).astype(BF16)
    col_x = remote(call.at[h, x], call.at[h, x], c_send.at[0], c_recv.at[0], xp)
    col_s = remote(call.at[h, x], call.at[h, x], c_send.at[1], c_recv.at[1], sib)
    col_x.start()
    col_s.start()
    sends += [col_x, col_s]
    col_x.wait_recv()
    other = call.at[h, 1 - x]
    col_f = remote(other, other, c_send.at[2], c_recv.at[2], sib)
    col_f.start()
    sends.append(col_f)

    gc = []
    for c in range(2):
        for i in range(k7):
            ag[c * k7 + i].wait_recv()
        gc.append(remote(dall.at[h, c], dall.at[h, c], gc_send.at[c], gc_recv.at[c], sib))
        gc[c].start()
    sends += gc

    col_s.wait_recv()
    col_f.wait_recv()
    for a in range(2):
        for b in range(2):
            col_out[:, b * BLK:(b + 1) * BLK, a * BLK:(a + 1) * BLK] = call[a, b]
    locs[3].wait()
    pr = dall.shape[4]
    for c in range(2):
        gc[c].wait_recv()
        for a in range(2):
            for b in range(2):
                rs = slice(b * BLK, (b + 1) * BLK)
                cs = slice(a * BLK, (a + 1) * BLK)
                diag_out[c, rs, cs] = d_v[c, rs, cs] - dall[a, c, b].reshape(n * pr, BLK)
    for c in sends:
        c.wait_send()


def fused(n, ainv, panel, upanel, dinv, pattern):
    w = ainv.shape[2]
    pr = BLK // n
    dma = pltpu.SemaphoreType.DMA
    hbm = pl.BlockSpec(memory_space=pltpu.HBM)
    vmem = pl.BlockSpec(memory_space=pltpu.VMEM)
    return pl.pallas_call(
        functools.partial(kernel, n),
        out_shape=(
            jax.ShapeDtypeStruct((2, w, w), BF16),
            jax.ShapeDtypeStruct((2, w, w), F32),
        ),
        in_specs=[hbm] * 5,
        out_specs=(vmem, vmem),
        scratch_shapes=[
            pltpu.SMEM((2, 2), jnp.int32),
            pltpu.VMEM((2, w, w), BF16),
            pltpu.VMEM((2, w, w), BF16),
            pltpu.VMEM((2, w, w), F32),
            pltpu.VMEM((2, w, w), BF16),
            pltpu.VMEM((2 * w, 2 * w), BF16),
            pltpu.VMEM((2 * w, 2 * w), BF16),
            pltpu.VMEM((2, 2 * w, BLK), F32),
            pltpu.VMEM((2 * w, BLK), F32),
            pltpu.VMEM((2, 2, BLK, BLK), F32),
            pltpu.VMEM((2, 2, n, pr, BLK), F32),
            pltpu.VMEM((2, BLK, BLK), F32),
            pltpu.VMEM((4 * n - 2, pr, BLK), F32),
            pltpu.VMEM((2, 2, 2, n, pr, BLK), F32),
            pltpu.VMEM((2, 2, 2, BLK, BLK), BF16),
            dma((5,)),
            dma((n,)), dma((n,)),
            dma((2,)), dma((2,)),
            dma, dma,
            dma((4 * n - 2,)), dma((4 * n - 2,)),
            dma((4 * n - 2,)), dma((4 * n - 2,)),
            dma((2,)), dma((2,)),
            dma((3,)), dma((3,)),
        ],
        compiler_params=pltpu.CompilerParams(
            collective_id=0, has_side_effects=True, vmem_limit_bytes=48 * 2**20),
        cost_estimate=pl.CostEstimate(
            flops=12 * w**3, bytes_accessed=12 * w * w, transcendentals=0),
    )(*(pltpu.with_memory_space_constraint(v, pltpu.HBM)
        for v in (ainv, panel, upanel, dinv, pattern)))


def complex_dot(left_re, left_im, right_re, right_im):
    real = jnp.dot(left_re, right_re, preferred_element_type=F32) - jnp.dot(
        left_im, right_im, preferred_element_type=F32
    )
    imag = jnp.dot(left_re, right_im, preferred_element_type=F32) + jnp.dot(
        left_im, right_re, preferred_element_type=F32
    )
    return (real, imag)


def upper_terms(up_full, column_full):
    hi = lax.Precision.HIGHEST
    d_re = jnp.dot(up_full[0], column_full[0], precision=hi) - jnp.dot(
        up_full[1], column_full[1], precision=hi
    )
    d_im = jnp.dot(up_full[0], column_full[1], precision=hi) + jnp.dot(
        up_full[1], column_full[0], precision=hi
    )
    return jnp.stack([d_re, d_im])


def general(ainv, panel, upanel, dinv, pattern):
    local_cols = ainv.shape[2]
    row_blocks = pattern.shape[0]
    col_blocks = pattern.shape[1]
    width = panel.shape[4]
    weights = pattern.astype(BF16)
    masked = (
        ainv.reshape(2, row_blocks, BLK, col_blocks, BLK) * weights[None, :, None, :, None]
    ).reshape(ainv.shape)
    gathered = lax.all_gather(panel, "prow", axis=2, tiled=True).reshape(2, local_cols, width)
    real, imag = complex_dot(masked[0], masked[1], gathered[0], gathered[1])
    column_full = lax.psum(jnp.stack([-real, -imag]), "pcol")
    column = column_full.astype(BF16)
    total = lax.psum(upper_terms(upanel.astype(F32), column_full), "prow")
    return (column, dinv - total)


def solution(mesh):
    n = mesh.shape["prow"]

    def per_device(ainv, panel, upanel, dinv, pattern):
        square = ainv.shape[1:] == (2 * BLK, 2 * BLK) and panel.shape[4] == 2 * BLK
        if n == 4 and mesh.shape["pcol"] == 4 and square:
            return fused(n, ainv, panel, upanel, dinv, pattern)
        return general(ainv, panel, upanel, dinv, pattern)

    in_specs = (
        P("pole", "prow", "pcol"),
        P("pole", "pcol", "prow", None, None),
        P("pole", None, "prow"),
        P("pole", None, None),
        P("prow", "pcol"),
    )
    out_specs = (P("pole", "prow", None), P("pole", None, None))
    return jax.shard_map(
        per_device, mesh=mesh, in_specs=in_specs, out_specs=out_specs, check_vma=False
    )
```
